32 devices in a mesh: groups: 2 (over y), row: 8 (over z, x), col: 2 (over core).
Axes of the slice: x: 2, y: 2, z: 4, core: 2. Of those that a mesh axis runs over, the one named last changes fastest.
Arguments:
- tokens: bfloat16 [512, 8192], P(('groups', 'col'), 'row'), parts along dimension 0, may hold values from -6 to 6
- gate_weight: bfloat16 [16384, 26624], P(('groups', 'row'), 'col'), parts along dimension 0, may hold values from -6 to 6
- up_weight: bfloat16 [8192, 26624], P('row', 'col'), may hold values from -6 to 6
- gate_up_left: bfloat16 [4, 8192, 128], P(None, 'row'), may hold values from -6 to 6
- gate_up_right: bfloat16 [4, 2, 64, 26624], P(None, None, None, ('col', 'row')), may hold values from -0.3984375 to 0.3984375
- adapter_ids: int32 [4], P('groups'), parts along dimension 0, may hold values from 0 to 3
Outputs:
- gate_merged: bfloat16 [16384, 26624], P(('groups', 'row'), 'col'), parts along dimension 0
- hidden: bfloat16 [512, 26624], P('groups', ('col', 'row')), parts along dimension 0
The draws below stay inside these ranges and needn't reach their ends.
There are 2 independent parts, one for each index of `groups`. The reference program is written for one: setup_inputs(seed, part) draws one part's arguments, and reference() takes and returns one part's arrays. A program takes and returns all parts, laid end to end along the dimension named above; an argument that names none is the same for every part. Nothing has to cross between parts.
All inputs are finite; a program needn't handle non-finite values.
Results may differ from the reference program's by a relative error of at most 0.005.
Values may be sent and summed in bfloat16 or wider, within the bound.
A program may use at most 256 MiB of HBM per device.

```python
import jax
import jax.numpy as jnp

MODEL_WIDTH = 8192
HIDDEN_UNITS = 26624
ADAPTER_RANK = 64
ADAPTER_SETS = 4
TOKENS = 256


def level_of(own_key, shape, cuts, least, high):
    def one(axis_at, blocks):
        steps = jax.random.uniform(jax.random.fold_in(jax.random.fold_in(own_key, 6), axis_at), (blocks,), jnp.float32, least / len(cuts), high / len(cuts))
        return jnp.repeat(jnp.exp(steps), shape[axis_at] // blocks).reshape((-1,) + (1,) * (len(shape) - axis_at - 1))

    loudness = one(*cuts[0])
    for cut in cuts[1:]:
        loudness = loudness * one(*cut)
    return loudness


def centred(own_key, shape, deviation, reach, pieces=(), held_as=jnp.bfloat16):
    gain = level_of(own_key, shape, pieces, -0.22, 0.18) if pieces else 1.0
    drawn = jax.random.normal(own_key, shape, jnp.float32) * deviation * gain
    return jnp.minimum(jnp.maximum(drawn, -reach), reach).astype(held_as)


def setup_inputs(seed: int = 0, part: int = 0) -> dict:
    arg_keys = jax.random.split(jax.random.key(seed), 7)
    part_keys = jax.random.split(jax.random.fold_in(arg_keys[6], part), 7)
    return {
        "tokens": centred(part_keys[0], (TOKENS, MODEL_WIDTH), 1.0, 6.0, ((0, 2), (1, 8))),
        "gate_weight": centred(part_keys[1], (MODEL_WIDTH, HIDDEN_UNITS), 1.0, 6.0, ((0, 8), (1, 2))),
        "up_weight": centred(arg_keys[2], (MODEL_WIDTH, HIDDEN_UNITS), 1.0, 6.0, ((0, 8), (1, 2))),
        "gate_up_left": centred(arg_keys[3], (ADAPTER_SETS, MODEL_WIDTH, 2 * ADAPTER_RANK), 1.0, 6.0, ((1, 8),)),
        "gate_up_right": centred(arg_keys[4], (ADAPTER_SETS, 2, ADAPTER_RANK, HIDDEN_UNITS), 0.0625, 0.3984375, ((3, 16),)),
        "adapter_ids": jax.random.randint(part_keys[5], (2,), 0, ADAPTER_SETS).astype(jnp.int32),
    }


def merge_panel(weight, left_panel, right_panel):
    update = jnp.dot(left_panel, right_panel, preferred_element_type=jnp.float32)
    return (weight.astype(jnp.float32) + update).astype(jnp.bfloat16)


def reference(tokens, gate_weight, up_weight, gate_up_left, gate_up_right, adapter_ids):
    scale_factor = float(MODEL_WIDTH) ** -0.5
    old_id = adapter_ids[0]
    new_id = adapter_ids[1]
    incoming_left = gate_up_left[new_id]
    outgoing_left = gate_up_left[old_id]
    gate_left_panel = jnp.concatenate([incoming_left[:, :ADAPTER_RANK], -outgoing_left[:, :ADAPTER_RANK]], axis=1)
    gate_right = jnp.concatenate([gate_up_right[new_id, 0], gate_up_right[old_id, 0]], axis=0)
    gate_merged = merge_panel(gate_weight, gate_left_panel, gate_right)
    gate_value = jnp.dot(tokens, gate_merged, preferred_element_type=jnp.float32) * scale_factor
    low_rank_term = (jnp.dot(tokens, incoming_left[:, ADAPTER_RANK:], preferred_element_type=jnp.float32) * scale_factor).astype(jnp.bfloat16)
    up_value = jnp.dot(tokens, up_weight, preferred_element_type=jnp.float32) * scale_factor
    up_value = up_value + jnp.dot(low_rank_term, gate_up_right[new_id, 1], preferred_element_type=jnp.float32)
    hidden = (jax.nn.silu(gate_value) * up_value).astype(jnp.bfloat16)
    return gate_merged, hidden
```

```python
import functools

import jax
import jax.numpy as jnp
from jax import lax
from jax.experimental import pallas as pl
from jax.experimental.pallas import tpu as pltpu
from jax.sharding import PartitionSpec as P


def merge_panel(weight, left_panel, right_panel):
    update = jnp.dot(left_panel, right_panel, preferred_element_type=jnp.float32)
    return (weight.astype(jnp.float32) + update).astype(jnp.bfloat16)


def choose(index, values):
    result = jnp.int32(values[-1])
    for at in range(len(values) - 2, -1, -1):
        result = jnp.where(index == at, jnp.int32(values[at]), result)
    return result


def chunks(width, step):
    return [(at, min(step, width - at)) for at in range(0, width, step)]


def scatter_kernel(
    line, tok_ref, up_ref, gate_ref, out_ref,
    wbuf, send_x, recv_x, own, recv_z,
    wsem, sx_sem, rx_sem, sz_sem, rz_sem,
):
    tokens, block = send_x.shape[1:]
    row = lax.axis_index("row")
    z = row // 2
    x = row % 2
    partner = z * 2 + (1 - x)
    terms = (up_ref, gate_ref)
    steps = 2 * line
    slots = wbuf.shape[0]
    orders = [sorted(range(line), key=lambda d: (-abs(d - at), d)) for at in range(line)]
    zd = [choose(z, [orders[at][j] for at in range(line)]) for j in range(line)]

    def tile_copy(index):
        step, mine = index // 2, index % 2
        column = zd[step % line] * 2 + (x if mine else 1 - x)
        source = terms[step // line].at[:, pl.ds(pl.multiple_of(column * block, 128), block)]
        return pltpu.make_async_copy(source, wbuf.at[index % slots], wsem.at[index % slots])

    for index in range(slots):
        tile_copy(index).start()

    barrier = pltpu.get_barrier_semaphore()
    pl.semaphore_signal(barrier, inc=1, device_id={"row": partner})

    @pl.when(z > 0)
    def _():
        pl.semaphore_signal(barrier, inc=1, device_id={"row": row - 2})

    @pl.when(z < line - 1)
    def _():
        pl.semaphore_signal(barrier, inc=1, device_id={"row": row + 2})

    pl.semaphore_wait(barrier, 1 + jnp.where(z > 0, 1, 0) + jnp.where(z < line - 1, 1, 0))

    def multiply(index, store):
        tile_copy(index).wait()
        slot = index % slots
        whole = block // 256

        def piece(columns):
            store(columns, jnp.dot(
                tok_ref[...], wbuf[slot, :, columns], preferred_element_type=jnp.float32
            ))

        @pl.loop(0, whole)
        def _(at):
            piece(pl.ds(pl.multiple_of(at * 256, 256), 256))

        if block % 256:
            piece(pl.ds(whole * 256, block % 256))
        if index + slots < 2 * steps:
            tile_copy(index + slots).start()

    def x_copy(step):
        return pltpu.make_async_remote_copy(
            src_ref=send_x.at[step], dst_ref=recv_x.at[step],
            send_sem=sx_sem.at[step], recv_sem=rx_sem.at[step],
            device_id={"row": partner},
        )

    def z_copy(step):
        term, j = step // line, step % line
        up = zd[j] > z
        target = jnp.where(up, row + 2, row - 2)
        at_end = jnp.logical_and(jnp.logical_not(up), zd[j] == z - 1)
        slot = term * (line + 1) + jnp.where(at_end, line, zd[j])
        return pltpu.make_async_remote_copy(
            src_ref=recv_x.at[step], dst_ref=recv_z.at[slot],
            send_sem=sz_sem.at[step], recv_sem=rz_sem.at[slot],
            device_id={"row": target},
        )

    def wait_z(slot):
        pltpu.make_async_remote_copy(
            src_ref=recv_z.at[slot], dst_ref=recv_z.at[slot],
            send_sem=sz_sem.at[0], recv_sem=rz_sem.at[slot],
            device_id={"row": partner},
        ).wait_recv()

    def produce(step):
        def to_send(columns, value):
            send_x[step, :, columns] = value.astype(jnp.bfloat16)

        def to_own(columns, value):
            own[step, :, columns] = value

        multiply(2 * step, to_send)
        x_copy(step).start()
        multiply(2 * step + 1, to_own)

    def add_rows(step, slot):
        @pl.loop(0, tokens // 16)
        def _(at):
            rows = pl.ds(pl.multiple_of(at * 16, 16), 16)
            own[step, rows, :] = own[step, rows, :] + recv_z[slot, rows, :].astype(jnp.float32)

    def finish(step):
        term, j = step // line, step % line
        if j < line - 1:
            inner = jnp.logical_or(
                jnp.logical_and(zd[j] > z, z > 0), jnp.logical_and(zd[j] < z, z < line - 1)
            )
            slot = term * (line + 1) + zd[j]

            @pl.when(inner)
            def _():
                wait_z(slot)
                add_rows(step, slot)

            x_copy(step).wait_recv()

            @pl.loop(0, tokens // 16)
            def _(at):
                rows = pl.ds(pl.multiple_of(at * 16, 16), 16)
                total = own[step, rows, :] + recv_x[step, rows, :].astype(jnp.float32)
                recv_x[step, rows, :] = total.astype(jnp.bfloat16)

            z_copy(step).start()
        else:
            x_copy(step).wait_recv()

            @pl.when(z > 0)
            def _():
                slot = term * (line + 1) + z
                wait_z(slot)
                add_rows(step, slot)

            @pl.when(z < line - 1)
            def _():
                slot = term * (line + 1) + line
                wait_z(slot)
                add_rows(step, slot)

            @pl.loop(0, tokens // 16)
            def _(at):
                rows = pl.ds(pl.multiple_of(at * 16, 16), 16)
                out_ref[term, rows, :] = own[step, rows, :] + recv_x[step, rows, :].astype(jnp.float32)

    for step in range(line):
        produce(step)
    done = 0
    for step in range(line, steps):
        finish(done)
        done += 1
        produce(step)
    for step in range(done, steps):
        finish(step)
    for step in range(steps):
        x_copy(step).wait_send()
        if step % line < line - 1:
            z_copy(step).wait_send()


def reduce_terms(tokens, up_weight, gate_weight, rows):
    count, width = tokens.shape
    block = up_weight.shape[1] // rows
    line = rows // 2
    steps = 2 * line
    return pl.pallas_call(
        functools.partial(scatter_kernel, line),
        out_shape=jax.ShapeDtypeStruct((2, count, block), jnp.float32),
        in_specs=[
            pl.BlockSpec(memory_space=pltpu.VMEM),
            pl.BlockSpec(memory_space=pl.ANY),
            pl.BlockSpec(memory_space=pl.ANY),
        ],
        out_specs=pl.BlockSpec(memory_space=pltpu.VMEM),
        scratch_shapes=[
            pltpu.VMEM((3, width, block), jnp.bfloat16),
            pltpu.VMEM((steps, count, block), jnp.bfloat16),
            pltpu.VMEM((steps, count, block), jnp.bfloat16),
            pltpu.VMEM((steps, count, block), jnp.float32),
            pltpu.VMEM((2 * (line + 1), count, block), jnp.bfloat16),
            pltpu.SemaphoreType.DMA((3,)),
            pltpu.SemaphoreType.DMA((steps,)),
            pltpu.SemaphoreType.DMA((steps,)),
            pltpu.SemaphoreType.DMA((steps,)),
            pltpu.SemaphoreType.DMA((2 * (line + 1),)),
        ],
        compiler_params=pltpu.CompilerParams(
            collective_id=0, has_side_effects=True, vmem_limit_bytes=56 * 2**20
        ),
        cost_estimate=pl.CostEstimate(
            flops=4 * count * width * block * rows,
            bytes_accessed=4 * width * block * rows,
            transcendentals=0,
        ),
    )(tokens, up_weight, gate_weight)


def per_device(tokens, gate_weight, up_weight, gate_up_left, gate_up_right, adapter_ids):
    rank = gate_up_right.shape[2]
    rows = lax.axis_size("row")
    old_id = adapter_ids[0]
    new_id = adapter_ids[1]
    incoming_left = gate_up_left[new_id]
    outgoing_left = gate_up_left[old_id]
    gate_left_panel = jnp.concatenate(
        [incoming_left[:, :rank], -outgoing_left[:, :rank]], axis=1
    )
    right_chosen = jnp.concatenate([gate_up_right[new_id, 0], gate_up_right[old_id, 0]], axis=0)
    all_tokens = lax.all_gather(tokens, "col", axis=0, tiled=True)
    right_all = lax.all_gather(right_chosen, "row", axis=1, tiled=True)
    gate_merged = merge_panel(gate_weight, gate_left_panel, right_all)
    scale = float(all_tokens.shape[1] * rows) ** (-0.5)
    count = all_tokens.shape[0]
    block = up_weight.shape[1] // rows
    if rows == 8 and block % 128 == 0 and count % 16 == 0:
        panels = jnp.concatenate([gate_left_panel, incoming_left[:, rank:]], axis=1)
        low = lax.psum(
            jnp.dot(all_tokens, panels, preferred_element_type=jnp.float32), "row"
        )
        sums = reduce_terms(all_tokens, up_weight, gate_weight, rows)
        gate_low = jnp.dot(
            low[:, : 2 * rank], right_chosen.astype(jnp.float32),
            precision=lax.Precision.HIGHEST, preferred_element_type=jnp.float32,
        )
        gate_value = (sums[1] + gate_low) * scale
        up_base = sums[0] * scale
        low_term = (low[:, 2 * rank :] * scale).astype(jnp.bfloat16)
    else:
        low = lax.psum(
            jnp.dot(all_tokens, incoming_left[:, rank:], preferred_element_type=jnp.float32), "row"
        )
        low_term = (low * scale).astype(jnp.bfloat16)
        contract = (((0,), (1,)), ((), ()))
        gate_term = lax.dot_general(
            gate_merged, all_tokens, contract, preferred_element_type=jnp.float32
        )
        up_term = lax.dot_general(
            up_weight, all_tokens, contract, preferred_element_type=jnp.float32
        )
        sums = lax.psum_scatter(
            jnp.concatenate([gate_term, up_term], axis=1), "row", scatter_dimension=0, tiled=True
        )
        gate_value = sums[:, :count].T * scale
        up_base = sums[:, count:].T * scale
    up_value = up_base + jnp.dot(
        low_term, gate_up_right[new_id, 1], preferred_element_type=jnp.float32
    )
    hidden = (jax.nn.silu(gate_value) * up_value).astype(jnp.bfloat16)
    return (gate_merged, hidden)


def solution(mesh):
    return jax.shard_map(
        per_device,
        mesh=mesh,
        in_specs=(
            P(("groups", "col"), "row"),
            P(("groups", "row"), "col"),
            P("row", "col"),
            P(None, "row", None),
            P(None, None, None, ("col", "row")),
            P("groups"),
        ),
        out_specs=(P(("groups", "row"), "col"), P("groups", ("col", "row"))),
        check_vma=False,
    )
```

```python
import functools

import jax
import jax.numpy as jnp
from jax import lax
from jax.experimental import pallas as pl
from jax.experimental.pallas import tpu as pltpu
from jax.sharding import PartitionSpec as P


def merge_panel(weight, left_panel, right_panel):
    update = jnp.dot(left_panel, right_panel, preferred_element_type=jnp.float32)
    return (weight.astype(jnp.float32) + update).astype(jnp.bfloat16)


def choose(index, values):
    result = jnp.int32(values[-1])
    for at in range(len(values) - 2, -1, -1):
        result = jnp.where(index == at, jnp.int32(values[at]), result)
    return result


def scatter_kernel(
    line, tok_ref, up_ref, gate_ref, right_ref, out_ref, hop_ref, panel_ref,
    wbuf, send_x, recv_x, own, recv_z,
    wsem, sx_sem, rx_sem, sz_sem, rz_sem,
    own_sem, pair_sem, up_sem, down_sem, panel_sem,
):
    tokens, block = send_x.shape[1:]
    row = lax.axis_index("row")
    z = row // 2
    x = row % 2
    partner = z * 2 + (1 - x)
    terms = (up_ref, gate_ref)
    steps = 2 * line
    slots = wbuf.shape[0]
    orders = [sorted(range(line), key=lambda d: (-abs(d - at), d)) for at in range(line)]
    zd = [choose(z, [orders[at][j] for at in range(line)]) for j in range(line)]

    def tile_copy(index):
        step, mine = index // 2, index % 2
        column = zd[step % line] * 2 + (x if mine else 1 - x)
        source = terms[step // line].at[:, pl.ds(pl.multiple_of(column * block, 128), block)]
        return pltpu.make_async_copy(source, wbuf.at[index % slots], wsem.at[index % slots])

    for index in range(slots):
        tile_copy(index).start()

    barrier = pltpu.get_barrier_semaphore()
    pl.semaphore_signal(barrier, inc=1, device_id={"row": partner})

    @pl.when(z > 0)
    def _():
        pl.semaphore_signal(barrier, inc=1, device_id={"row": row - 2})

    @pl.when(z < line - 1)
    def _():
        pl.semaphore_signal(barrier, inc=1, device_id={"row": row + 2})

    pl.semaphore_wait(barrier, 1 + jnp.where(z > 0, 1, 0) + jnp.where(z < line - 1, 1, 0))

    def panel_at(first, width):
        return panel_ref.at[:, pl.ds(pl.multiple_of(first * block, 128), width * block)]

    own_panel = pltpu.make_async_copy(right_ref, panel_at(row, 1), own_sem)
    own_panel.start()

    def pair_copy(owner):
        return pltpu.make_async_remote_copy(
            src_ref=right_ref, dst_ref=panel_at(owner, 1),
            send_sem=pair_sem.at[0], recv_sem=pair_sem.at[1],
            device_id={"row": partner},
        )

    pair_copy(row).start()

    def panel_copy(owner, upward):
        sems = up_sem if upward else down_sem
        return pltpu.make_async_remote_copy(
            src_ref=panel_at(owner * 2, 2), dst_ref=panel_at(owner * 2, 2),
            send_sem=sems.at[owner], recv_sem=panel_sem.at[owner],
            device_id={"row": row + 2 if upward else row - 2},
        )

    def gather(hop):
        if hop == 0:
            own_panel.wait()
            pair_copy(partner).wait_recv()

        @pl.when(z - hop >= 0)
        def _():
            if hop:
                panel_copy(z - hop, True).wait_recv()

            @pl.when(z < line - 1)
            def _():
                panel_copy(z - hop, True).start()

        @pl.when(z + hop < line)
        def _():
            if hop:
                panel_copy(z + hop, False).wait_recv()

            @pl.when(z > 0)
            def _():
                panel_copy(z + hop, False).start()

    def gather_end():
        pair_copy(row).wait_send()
        for hop in range(line):
            @pl.when(jnp.logical_and(z - hop >= 0, z < line - 1))
            def _():
                panel_copy(z - hop, True).wait_send()

            @pl.when(jnp.logical_and(z + hop < line, z > 0))
            def _():
                panel_copy(z + hop, False).wait_send()

    def multiply(index, store):
        tile_copy(index).wait()
        slot = index % slots
        whole = block // 256

        def piece(columns):
            store(columns, jnp.dot(
                tok_ref[...], wbuf[slot, :, columns], preferred_element_type=jnp.float32
            ))

        @pl.loop(0, whole)
        def _(at):
            piece(pl.ds(pl.multiple_of(at * 256, 256), 256))

        if block % 256:
            piece(pl.ds(whole * 256, block % 256))
        if index + slots < 2 * steps:
            tile_copy(index + slots).start()

    def x_copy(step):
        return pltpu.make_async_remote_copy(
            src_ref=send_x.at[step], dst_ref=recv_x.at[step],
            send_sem=sx_sem.at[step], recv_sem=rx_sem.at[step],
            device_id={"row": partner},
        )

    def z_copy(step):
        term, j = step // line, step % line
        up = zd[j] > z
        target = jnp.where(up, row + 2, row - 2)
        at_end = jnp.logical_and(jnp.logical_not(up), zd[j] == z - 1)
        slot = term * (line + 1) + jnp.where(at_end, line, zd[j])
        return pltpu.make_async_remote_copy(
            src_ref=recv_x.at[step], dst_ref=recv_z.at[slot],
            send_sem=sz_sem.at[step], recv_sem=rz_sem.at[slot],
            device_id={"row": target},
        )

    def wait_z(slot):
        pltpu.make_async_remote_copy(
            src_ref=recv_z.at[slot], dst_ref=recv_z.at[slot],
            send_sem=sz_sem.at[0], recv_sem=rz_sem.at[slot],
            device_id={"row": partner},
        ).wait_recv()

    def produce(step):
        def to_send(columns, value):
            send_x[step, :, columns] = value.astype(jnp.bfloat16)

        def to_own(columns, value):
            own[step, :, columns] = value

        multiply(2 * step, to_send)
        x_copy(step).start()
        multiply(2 * step + 1, to_own)

    def last_hop(j):
        return jnp.logical_or(zd[j] == z + 1, zd[j] == z - 1)

    def add_rows(step, slot):
        @pl.loop(0, tokens // 16)
        def _(at):
            rows = pl.ds(pl.multiple_of(at * 16, 16), 16)
            own[step, rows, :] = own[step, rows, :] + recv_z[slot, rows, :].astype(jnp.float32)

    def finish(step):
        term, j = step // line, step % line
        if j < line - 1:
            inner = jnp.logical_or(
                jnp.logical_and(zd[j] > z, z > 0), jnp.logical_and(zd[j] < z, z < line - 1)
            )
            slot = term * (line + 1) + zd[j]

            @pl.when(inner)
            def _():
                wait_z(slot)
                add_rows(step, slot)

            x_copy(step).wait_recv()

            @pl.loop(0, tokens // 16)
            def _(at):
                rows = pl.ds(pl.multiple_of(at * 16, 16), 16)
                total = own[step, rows, :] + recv_x[step, rows, :].astype(jnp.float32)
                recv_x[step, rows, :] = total.astype(jnp.bfloat16)

            if term == 0:
                z_copy(step).start()
            else:
                @pl.when(last_hop(j))
                def _():
                    side = jnp.where(zd[j] > z, 0, 1)

                    @pl.loop(0, tokens // 16)
                    def _(at):
                        rows = pl.ds(pl.multiple_of(at * 16, 16), 16)
                        hop_ref[side, rows, :] = recv_x[step, rows, :]

                @pl.when(jnp.logical_not(last_hop(j)))
                def _():
                    z_copy(step).start()
        else:
            x_copy(step).wait_recv()

            if term == 0:
                @pl.when(z > 0)
                def _():
                    slot = term * (line + 1) + z
                    wait_z(slot)
                    add_rows(step, slot)

                @pl.when(z < line - 1)
                def _():
                    slot = term * (line + 1) + line
                    wait_z(slot)
                    add_rows(step, slot)

            @pl.loop(0, tokens // 16)
            def _(at):
                rows = pl.ds(pl.multiple_of(at * 16, 16), 16)
                out_ref[term, rows, :] = own[step, rows, :] + recv_x[step, rows, :].astype(jnp.float32)

    for step in range(line):
        produce(step)
        if step == 0:
            gather(0)
    done = 0
    for step in range(line, steps):
        finish(done)
        done += 1
        produce(step)
        if done < line:
            gather(done)
    for step in range(done, steps):
        finish(step)
    for step in range(steps):
        x_copy(step).wait_send()
        if step < line - 1:
            z_copy(step).wait_send()
        elif line <= step < steps - 1:
            @pl.when(jnp.logical_not(last_hop(step - line)))
            def _():
                z_copy(step).wait_send()
    gather_end()


def reduce_terms(tokens, up_weight, gate_weight, right, rows):
    count, width = tokens.shape
    block = up_weight.shape[1] // rows
    line = rows // 2
    steps = 2 * line
    return pl.pallas_call(
        functools.partial(scatter_kernel, line),
        out_shape=(
            jax.ShapeDtypeStruct((2, count, block), jnp.float32),
            jax.ShapeDtypeStruct((2, count, block), jnp.bfloat16),
            jax.ShapeDtypeStruct((right.shape[0], rows * block), jnp.bfloat16),
        ),
        in_specs=[
            pl.BlockSpec(memory_space=pltpu.VMEM),
            pl.BlockSpec(memory_space=pl.ANY),
            pl.BlockSpec(memory_space=pl.ANY),
            pl.BlockSpec(memory_space=pl.ANY),
        ],
        out_specs=(
            pl.BlockSpec(memory_space=pltpu.VMEM),
            pl.BlockSpec(memory_space=pltpu.VMEM),
            pl.BlockSpec(memory_space=pl.ANY),
        ),
        scratch_shapes=[
            pltpu.VMEM((3, width, block), jnp.bfloat16),
            pltpu.VMEM((steps, count, block), jnp.bfloat16),
            pltpu.VMEM((steps, count, block), jnp.bfloat16),
            pltpu.VMEM((steps, count, block), jnp.float32),
            pltpu.VMEM((2 * (line + 1), count, block), jnp.bfloat16),
            pltpu.SemaphoreType.DMA((3,)),
            pltpu.SemaphoreType.DMA((steps,)),
            pltpu.SemaphoreType.DMA((steps,)),
            pltpu.SemaphoreType.DMA((steps,)),
            pltpu.SemaphoreType.DMA((2 * (line + 1),)),
            pltpu.SemaphoreType.DMA,
            pltpu.SemaphoreType.DMA((2,)),
            pltpu.SemaphoreType.DMA((line,)),
            pltpu.SemaphoreType.DMA((line,)),
            pltpu.SemaphoreType.DMA((line,)),
        ],
        compiler_params=pltpu.CompilerParams(
            collective_id=0, has_side_effects=True, vmem_limit_bytes=56 * 2**20
        ),
        cost_estimate=pl.CostEstimate(
            flops=4 * count * width * block * rows,
            bytes_accessed=4 * width * block * rows,
            transcendentals=0,
        ),
    )(tokens, up_weight, gate_weight, right)


def per_device(tokens, gate_weight, up_weight, gate_up_left, gate_up_right, adapter_ids):
    rank = gate_up_right.shape[2]
    rows = lax.axis_size("row")
    old_id = adapter_ids[0]
    new_id = adapter_ids[1]
    incoming_left = gate_up_left[new_id]
    outgoing_left = gate_up_left[old_id]
    gate_left_panel = jnp.concatenate(
        [incoming_left[:, :rank], -outgoing_left[:, :rank]], axis=1
    )
    right_chosen = jnp.concatenate([gate_up_right[new_id, 0], gate_up_right[old_id, 0]], axis=0)
    all_tokens = lax.all_gather(tokens, "col", axis=0, tiled=True)
    scale = float(all_tokens.shape[1] * rows) ** (-0.5)
    count = all_tokens.shape[0]
    block = up_weight.shape[1] // rows
    if rows == 8 and block % 128 == 0 and count % 16 == 0:
        panels = jnp.concatenate([gate_left_panel, incoming_left[:, rank:]], axis=1)
        low = lax.psum(
            jnp.dot(all_tokens, panels, preferred_element_type=jnp.float32), "row"
        )
        sums, hops, right_all = reduce_terms(
            all_tokens, up_weight, gate_weight, right_chosen, rows
        )
        below = lax.ppermute(hops[0], "row", [(at, at + 2) for at in range(rows - 2)])
        above = lax.ppermute(hops[1], "row", [(at + 2, at) for at in range(rows - 2)])
        gate_merged = merge_panel(gate_weight, gate_left_panel, right_all)
        gate_low = jnp.dot(
            low[:, : 2 * rank], right_chosen.astype(jnp.float32),
            precision=lax.Precision.HIGHEST, preferred_element_type=jnp.float32,
        )
        gate_sum = sums[1] + below.astype(jnp.float32) + above.astype(jnp.float32)
        gate_value = (gate_sum + gate_low) * scale
        up_base = sums[0] * scale
        low_term = (low[:, 2 * rank :] * scale).astype(jnp.bfloat16)
    else:
        right_all = lax.all_gather(right_chosen, "row", axis=1, tiled=True)
        gate_merged = merge_panel(gate_weight, gate_left_panel, right_all)
        low = lax.psum(
            jnp.dot(all_tokens, incoming_left[:, rank:], preferred_element_type=jnp.float32), "row"
        )
        low_term = (low * scale).astype(jnp.bfloat16)
        contract = (((0,), (1,)), ((), ()))
        gate_term = lax.dot_general(
            gate_merged, all_tokens, contract, preferred_element_type=jnp.float32
        )
        up_term = lax.dot_general(
            up_weight, all_tokens, contract, preferred_element_type=jnp.float32
        )
        sums = lax.psum_scatter(
            jnp.concatenate([gate_term, up_term], axis=1), "row", scatter_dimension=0, tiled=True
        )
        gate_value = sums[:, :count].T * scale
        up_base = sums[:, count:].T * scale
    up_value = up_base + jnp.dot(
        low_term, gate_up_right[new_id, 1], preferred_element_type=jnp.float32
    )
    hidden = (jax.nn.silu(gate_value) * up_value).astype(jnp.bfloat16)
    return (gate_merged, hidden)


def solution(mesh):
    return jax.shard_map(
        per_device,
        mesh=mesh,
        in_specs=(
            P(("groups", "col"), "row"),
            P(("groups", "row"), "col"),
            P("row", "col"),
            P(None, "row", None),
            P(None, None, None, ("col", "row")),
            P("groups"),
        ),
        out_specs=(P(("groups", "row"), "col"), P("groups", ("col", "row"))),
        check_vma=False,
    )
```

```python
import functools

import jax
import jax.numpy as jnp
from jax import lax
from jax.experimental import pallas as pl
from jax.experimental.pallas import tpu as pltpu
from jax.sharding import PartitionSpec as P


def merge_panel(weight, left_panel, right_panel):
    update = jnp.dot(left_panel, right_panel, preferred_element_type=jnp.float32)
    return (weight.astype(jnp.float32) + update).astype(jnp.bfloat16)


def choose(index, values):
    result = jnp.int32(values[-1])
    for at in range(len(values) - 2, -1, -1):
        result = jnp.where(index == at, jnp.int32(values[at]), result)
    return result


def scatter_kernel(
    line, tok_ref, up_ref, gate_ref, right_ref,
    out_ref, up_hop_ref, down_hop_ref, pair_hop_ref, panel_ref,
    wbuf, send_x, recv_x, own, recv_z,
    wsem, sx_sem, rx_sem, sz_sem, rz_sem,
    own_sem, pair_sem, up_sem, down_sem, panel_sem,
):
    tokens, block = send_x.shape[1:]
    row = lax.axis_index("row")
    z = row // 2
    x = row % 2
    partner = z * 2 + (1 - x)
    terms = (up_ref, gate_ref)
    steps = 2 * line
    slots = wbuf.shape[0]
    orders = [sorted(range(line), key=lambda d: (-abs(d - at), d)) for at in range(line)]
    zd = [choose(z, [orders[at][j] for at in range(line)]) for j in range(line)]

    def tile_copy(index):
        step, mine = index // 2, index % 2
        column = zd[step % line] * 2 + (x if mine else 1 - x)
        source = terms[step // line].at[:, pl.ds(pl.multiple_of(column * block, 128), block)]
        return pltpu.make_async_copy(source, wbuf.at[index % slots], wsem.at[index % slots])

    for index in range(slots):
        tile_copy(index).start()

    barrier = pltpu.get_barrier_semaphore()
    pl.semaphore_signal(barrier, inc=1, device_id={"row": partner})

    @pl.when(z > 0)
    def _():
        pl.semaphore_signal(barrier, inc=1, device_id={"row": row - 2})

    @pl.when(z < line - 1)
    def _():
        pl.semaphore_signal(barrier, inc=1, device_id={"row": row + 2})

    pl.semaphore_wait(barrier, 1 + jnp.where(z > 0, 1, 0) + jnp.where(z < line - 1, 1, 0))

    def panel_at(first, width):
        return panel_ref.at[:, pl.ds(pl.multiple_of(first * block, 128), width * block)]

    own_panel = pltpu.make_async_copy(right_ref, panel_at(row, 1), own_sem)
    own_panel.start()

    def pair_copy(owner):
        return pltpu.make_async_remote_copy(
            src_ref=right_ref, dst_ref=panel_at(owner, 1),
            send_sem=pair_sem.at[0], recv_sem=pair_sem.at[1],
            device_id={"row": partner},
        )

    pair_copy(row).start()

    def panel_copy(owner, upward):
        sems = up_sem if upward else down_sem
        return pltpu.make_async_remote_copy(
            src_ref=panel_at(owner * 2, 2), dst_ref=panel_at(owner * 2, 2),
            send_sem=sems.at[owner], recv_sem=panel_sem.at[owner],
            device_id={"row": row + 2 if upward else row - 2},
        )

    def gather(hop):
        if hop == 0:
            own_panel.wait()
            pair_copy(partner).wait_recv()

        @pl.when(z - hop >= 0)
        def _():
            if hop:
                panel_copy(z - hop, True).wait_recv()

            @pl.when(z < line - 1)
            def _():
                panel_copy(z - hop, True).start()

        @pl.when(z + hop < line)
        def _():
            if hop:
                panel_copy(z + hop, False).wait_recv()

            @pl.when(z > 0)
            def _():
                panel_copy(z + hop, False).start()

    def gather_end():
        pair_copy(row).wait_send()
        for hop in range(line):
            @pl.when(jnp.logical_and(z - hop >= 0, z < line - 1))
            def _():
                panel_copy(z - hop, True).wait_send()

            @pl.when(jnp.logical_and(z + hop < line, z > 0))
            def _():
                panel_copy(z + hop, False).wait_send()

    def multiply(index, store):
        tile_copy(index).wait()
        slot = index % slots
        whole = block // 256

        def piece(columns):
            store(columns, jnp.dot(
                tok_ref[...], wbuf[slot, :, columns], preferred_element_type=jnp.float32
            ))

        @pl.loop(0, whole)
        def _(at):
            piece(pl.ds(pl.multiple_of(at * 256, 256), 256))

        if block % 256:
            piece(pl.ds(whole * 256, block % 256))
        if index + slots < 2 * steps:
            tile_copy(index + slots).start()

    def x_copy(step):
        return pltpu.make_async_remote_copy(
            src_ref=send_x.at[step], dst_ref=recv_x.at[step],
            send_sem=sx_sem.at[step], recv_sem=rx_sem.at[step],
            device_id={"row": partner},
        )

    def z_copy(step):
        term, j = step // line, step % line
        up = zd[j] > z
        target = jnp.where(up, row + 2, row - 2)
        at_end = jnp.logical_and(jnp.logical_not(up), zd[j] == z - 1)
        slot = term * (line + 1) + jnp.where(at_end, line, zd[j])
        return pltpu.make_async_remote_copy(
            src_ref=recv_x.at[step], dst_ref=recv_z.at[slot],
            send_sem=sz_sem.at[step], recv_sem=rz_sem.at[slot],
            device_id={"row": target},
        )

    def wait_z(slot):
        pltpu.make_async_remote_copy(
            src_ref=recv_z.at[slot], dst_ref=recv_z.at[slot],
            send_sem=sz_sem.at[0], recv_sem=rz_sem.at[slot],
            device_id={"row": partner},
        ).wait_recv()

    def produce(step):
        def to_send(columns, value):
            send_x[step, :, columns] = value.astype(jnp.bfloat16)

        def to_own(columns, value):
            own[step, :, columns] = value

        def to_pair_hop(columns, value):
            pair_hop_ref[:, columns] = value.astype(jnp.bfloat16)

        def to_out(columns, value):
            out_ref[1, :, columns] = value

        if step < steps - 1:
            multiply(2 * step, to_send)
            x_copy(step).start()
            multiply(2 * step + 1, to_own)
        else:
            multiply(2 * step, to_pair_hop)
            multiply(2 * step + 1, to_out)

    def last_hop(j):
        return jnp.logical_or(zd[j] == z + 1, zd[j] == z - 1)

    def add_rows(step, slot):
        @pl.loop(0, tokens // 16)
        def _(at):
            rows = pl.ds(pl.multiple_of(at * 16, 16), 16)
            own[step, rows, :] = own[step, rows, :] + recv_z[slot, rows, :].astype(jnp.float32)

    def finish(step):
        term, j = step // line, step % line
        if j < line - 1:
            inner = jnp.logical_or(
                jnp.logical_and(zd[j] > z, z > 0), jnp.logical_and(zd[j] < z, z < line - 1)
            )
            slot = term * (line + 1) + zd[j]

            @pl.when(inner)
            def _():
                wait_z(slot)
                add_rows(step, slot)

            x_copy(step).wait_recv()

            @pl.loop(0, tokens // 16)
            def _(at):
                rows = pl.ds(pl.multiple_of(at * 16, 16), 16)
                total = own[step, rows, :] + recv_x[step, rows, :].astype(jnp.float32)
                recv_x[step, rows, :] = total.astype(jnp.bfloat16)

            if term == 0:
                z_copy(step).start()
            else:
                def keep(hop_ref):
                    @pl.loop(0, tokens // 16)
                    def _(at):
                        rows = pl.ds(pl.multiple_of(at * 16, 16), 16)
                        hop_ref[rows, :] = recv_x[step, rows, :]

                @pl.when(zd[j] == z + 1)
                def _():
                    keep(up_hop_ref)

                @pl.when(zd[j] == z - 1)
                def _():
                    keep(down_hop_ref)

                @pl.when(jnp.logical_not(last_hop(j)))
                def _():
                    z_copy(step).start()
        else:
            x_copy(step).wait_recv()

            @pl.when(z > 0)
            def _():
                slot = term * (line + 1) + z
                wait_z(slot)
                add_rows(step, slot)

            @pl.when(z < line - 1)
            def _():
                slot = term * (line + 1) + line
                wait_z(slot)
                add_rows(step, slot)

            @pl.loop(0, tokens // 16)
            def _(at):
                rows = pl.ds(pl.multiple_of(at * 16, 16), 16)
                out_ref[term, rows, :] = own[step, rows, :] + recv_x[step, rows, :].astype(jnp.float32)

    for step in range(line):
        produce(step)
        if step == 0:
            gather(0)
    done = 0
    for step in range(line, steps):
        finish(done)
        done += 1
        produce(step)
        if done < line:
            gather(done)
    for step in range(done, steps - 1):
        finish(step)
    for step in range(steps - 1):
        x_copy(step).wait_send()
        if step < line - 1:
            z_copy(step).wait_send()
        elif step >= line:
            @pl.when(jnp.logical_not(last_hop(step - line)))
            def _():
                z_copy(step).wait_send()
    gather_end()


def reduce_terms(tokens, up_weight, gate_weight, right, rows):
    count, width = tokens.shape
    block = up_weight.shape[1] // rows
    line = rows // 2
    steps = 2 * line
    return pl.pallas_call(
        functools.partial(scatter_kernel, line),
        out_shape=(
            jax.ShapeDtypeStruct((2, count, block), jnp.float32),
            jax.ShapeDtypeStruct((count, block), jnp.bfloat16),
            jax.ShapeDtypeStruct((count, block), jnp.bfloat16),
            jax.ShapeDtypeStruct((count, block), jnp.bfloat16),
            jax.ShapeDtypeStruct((right.shape[0], rows * block), jnp.bfloat16),
        ),
        in_specs=[
            pl.BlockSpec(memory_space=pltpu.VMEM),
            pl.BlockSpec(memory_space=pl.ANY),
            pl.BlockSpec(memory_space=pl.ANY),
            pl.BlockSpec(memory_space=pl.ANY),
        ],
        out_specs=(
            pl.BlockSpec(memory_space=pltpu.VMEM),
            pl.BlockSpec(memory_space=pltpu.VMEM),
            pl.BlockSpec(memory_space=pltpu.VMEM),
            pl.BlockSpec(memory_space=pltpu.VMEM),
            pl.BlockSpec(memory_space=pl.ANY),
        ),
        scratch_shapes=[
            pltpu.VMEM((3, width, block), jnp.bfloat16),
            pltpu.VMEM((steps, count, block), jnp.bfloat16),
            pltpu.VMEM((steps, count, block), jnp.bfloat16),
            pltpu.VMEM((steps, count, block), jnp.float32),
            pltpu.VMEM((2 * (line + 1), count, block), jnp.bfloat16),
            pltpu.SemaphoreType.DMA((3,)),
            pltpu.SemaphoreType.DMA((steps,)),
            pltpu.SemaphoreType.DMA((steps,)),
            pltpu.SemaphoreType.DMA((steps,)),
            pltpu.SemaphoreType.DMA((2 * (line + 1),)),
            pltpu.SemaphoreType.DMA,
            pltpu.SemaphoreType.DMA((2,)),
            pltpu.SemaphoreType.DMA((line,)),
            pltpu.SemaphoreType.DMA((line,)),
            pltpu.SemaphoreType.DMA((line,)),
        ],
        compiler_params=pltpu.CompilerParams(
            collective_id=0, has_side_effects=True, vmem_limit_bytes=56 * 2**20
        ),
        cost_estimate=pl.CostEstimate(
            flops=4 * count * width * block * rows,
            bytes_accessed=4 * width * block * rows,
            transcendentals=0,
        ),
    )(tokens, up_weight, gate_weight, right)


def per_device(tokens, gate_weight, up_weight, gate_up_left, gate_up_right, adapter_ids):
    rank = gate_up_right.shape[2]
    rows = lax.axis_size("row")
    old_id = adapter_ids[0]
    new_id = adapter_ids[1]
    incoming_left = gate_up_left[new_id]
    outgoing_left = gate_up_left[old_id]
    gate_left_panel = jnp.concatenate(
        [incoming_left[:, :rank], -outgoing_left[:, :rank]], axis=1
    )
    right_chosen = jnp.concatenate([gate_up_right[new_id, 0], gate_up_right[old_id, 0]], axis=0)
    all_tokens = lax.all_gather(tokens, "col", axis=0, tiled=True)
    scale = float(all_tokens.shape[1] * rows) ** (-0.5)
    count = all_tokens.shape[0]
    block = up_weight.shape[1] // rows
    if rows == 8 and block % 128 == 0 and count % 16 == 0:
        panels = jnp.concatenate([gate_left_panel, incoming_left[:, rank:]], axis=1)
        low = lax.psum(
            jnp.dot(all_tokens, panels, preferred_element_type=jnp.float32), "row"
        )
        sums, up_hop, down_hop, pair_hop, right_all = reduce_terms(
            all_tokens, up_weight, gate_weight, right_chosen, rows
        )
        below = lax.ppermute(up_hop, "row", [(at, at + 2) for at in range(rows - 2)])
        above = lax.ppermute(down_hop, "row", [(at + 2, at) for at in range(rows - 2)])
        beside = lax.ppermute(pair_hop, "row", [(at, at ^ 1) for at in range(rows)])
        gate_merged = merge_panel(gate_weight, gate_left_panel, right_all)
        gate_low = jnp.dot(
            low[:, : 2 * rank], right_chosen.astype(jnp.float32),
            precision=lax.Precision.HIGHEST, preferred_element_type=jnp.float32,
        )
        gate_sum = sums[1] + beside.astype(jnp.float32)
        gate_sum = gate_sum + below.astype(jnp.float32) + above.astype(jnp.float32)
        gate_value = (gate_sum + gate_low) * scale
        up_base = sums[0] * scale
        low_term = (low[:, 2 * rank :] * scale).astype(jnp.bfloat16)
    else:
        right_all = lax.all_gather(right_chosen, "row", axis=1, tiled=True)
        gate_merged = merge_panel(gate_weight, gate_left_panel, right_all)
        low = lax.psum(
            jnp.dot(all_tokens, incoming_left[:, rank:], preferred_element_type=jnp.float32), "row"
        )
        low_term = (low * scale).astype(jnp.bfloat16)
        contract = (((0,), (1,)), ((), ()))
        gate_term = lax.dot_general(
            gate_merged, all_tokens, contract, preferred_element_type=jnp.float32
        )
        up_term = lax.dot_general(
            up_weight, all_tokens, contract, preferred_element_type=jnp.float32
        )
        sums = lax.psum_scatter(
            jnp.concatenate([gate_term, up_term], axis=1), "row", scatter_dimension=0, tiled=True
        )
        gate_value = sums[:, :count].T * scale
        up_base = sums[:, count:].T * scale
    up_value = up_base + jnp.dot(
        low_term, gate_up_right[new_id, 1], preferred_element_type=jnp.float32
    )
    hidden = (jax.nn.silu(gate_value) * up_value).astype(jnp.bfloat16)
    return (gate_merged, hidden)


def solution(mesh):
    return jax.shard_map(
        per_device,
        mesh=mesh,
        in_specs=(
            P(("groups", "col"), "row"),
            P(("groups", "row"), "col"),
            P("row", "col"),
            P(None, "row", None),
            P(None, None, None, ("col", "row")),
            P("groups"),
        ),
        out_specs=(P(("groups", "row"), "col"), P("groups", ("col", "row"))),
        check_vma=False,
    )
```

```python
import functools

import jax
import jax.numpy as jnp
from jax import lax
from jax.experimental import pallas as pl
from jax.experimental.pallas import tpu as pltpu
from jax.sharding import PartitionSpec as P


def merge_panel(weight, left_panel, right_panel):
    update = jnp.dot(left_panel, right_panel, preferred_element_type=jnp.float32)
    return (weight.astype(jnp.float32) + update).astype(jnp.bfloat16)


def choose(index, values):
    result = jnp.int32(values[-1])
    for at in range(len(values) - 2, -1, -1):
        result = jnp.where(index == at, jnp.int32(values[at]), result)
    return result


def scatter_kernel(
    line, tok_ref, up_ref, gate_ref, right_ref,
    out_ref, up_hop_ref, down_hop_ref, pair_hop_ref, panel_ref,
    wbuf, send_x, recv_x, own, recv_z,
    wsem, sx_sem, rx_sem, sz_sem, rz_sem,
    own_sem, pair_sem, up_sem, down_sem, panel_sem,
):
    tokens, block = send_x.shape[1:]
    row = lax.axis_index("row")
    z = row // 2
    x = row % 2
    partner = z * 2 + (1 - x)
    terms = (up_ref, gate_ref)
    steps = 2 * line
    slots = wbuf.shape[0]
    orders = [sorted(range(line), key=lambda d: (-abs(d - at), d)) for at in range(line)]
    zd = [choose(z, [orders[at][j] for at in range(line)]) for j in range(line)]

    def tile_copy(index):
        step, mine = index // 2, index % 2
        column = zd[step % line] * 2 + (x if mine else 1 - x)
        source = terms[step // line].at[:, pl.ds(pl.multiple_of(column * block, 128), block)]
        return pltpu.make_async_copy(source, wbuf.at[index % slots], wsem.at[index % slots])

    for index in range(slots):
        tile_copy(index).start()

    barrier = pltpu.get_barrier_semaphore()
    pl.semaphore_signal(barrier, inc=1, device_id={"row": partner})

    @pl.when(z > 0)
    def _():
        pl.semaphore_signal(barrier, inc=1, device_id={"row": row - 2})

    @pl.when(z < line - 1)
    def _():
        pl.semaphore_signal(barrier, inc=1, device_id={"row": row + 2})

    pl.semaphore_wait(barrier, 1 + jnp.where(z > 0, 1, 0) + jnp.where(z < line - 1, 1, 0))

    def panel_at(first, width):
        return panel_ref.at[:, pl.ds(pl.multiple_of(first * block, 128), width * block)]

    own_panel = pltpu.make_async_copy(right_ref, panel_at(row, 1), own_sem)
    own_panel.start()

    def pair_copy(owner):
        return pltpu.make_async_remote_copy(
            src_ref=right_ref, dst_ref=panel_at(owner, 1),
            send_sem=pair_sem.at[0], recv_sem=pair_sem.at[1],
            device_id={"row": partner},
        )

    pair_copy(row).start()

    def panel_copy(owner, upward):
        sems = up_sem if upward else down_sem
        return pltpu.make_async_remote_copy(
            src_ref=panel_at(owner * 2, 2), dst_ref=panel_at(owner * 2, 2),
            send_sem=sems.at[owner], recv_sem=panel_sem.at[owner],
            device_id={"row": row + 2 if upward else row - 2},
        )

    def gather(hop):
        if hop == 0:
            own_panel.wait()
            pair_copy(partner).wait_recv()

        @pl.when(z - hop >= 0)
        def _():
            if hop:
                panel_copy(z - hop, True).wait_recv()

            @pl.when(z < line - 1)
            def _():
                panel_copy(z - hop, True).start()

        @pl.when(z + hop < line)
        def _():
            if hop:
                panel_copy(z + hop, False).wait_recv()

            @pl.when(z > 0)
            def _():
                panel_copy(z + hop, False).start()

    def gather_end():
        pair_copy(row).wait_send()
        for hop in range(line):
            @pl.when(jnp.logical_and(z - hop >= 0, z < line - 1))
            def _():
                panel_copy(z - hop, True).wait_send()

            @pl.when(jnp.logical_and(z + hop < line, z > 0))
            def _():
                panel_copy(z + hop, False).wait_send()

    def multiply(index, store):
        tile_copy(index).wait()
        slot = index % slots
        whole = block // 256

        def piece(columns):
            store(columns, jnp.dot(
                tok_ref[...], wbuf[slot, :, columns], preferred_element_type=jnp.float32
            ))

        @pl.loop(0, whole)
        def _(at):
            piece(pl.ds(pl.multiple_of(at * 256, 256), 256))

        if block % 256:
            piece(pl.ds(whole * 256, block % 256))
        if index + slots < 2 * steps:
            tile_copy(index + slots).start()

    def x_copy(step):
        return pltpu.make_async_remote_copy(
            src_ref=send_x.at[step], dst_ref=recv_x.at[step],
            send_sem=sx_sem.at[step], recv_sem=rx_sem.at[step],
            device_id={"row": partner},
        )

    def z_copy(step):
        term, j = step // line, step % line
        up = zd[j] > z
        target = jnp.where(up, row + 2, row - 2)
        at_end = jnp.logical_and(jnp.logical_not(up), zd[j] == z - 1)
        slot = term * (line + 1) + jnp.where(at_end, line, zd[j])
        return pltpu.make_async_remote_copy(
            src_ref=recv_x.at[step], dst_ref=recv_z.at[slot],
            send_sem=sz_sem.at[step], recv_sem=rz_sem.at[slot],
            device_id={"row": target},
        )

    def wait_z(slot):
        pltpu.make_async_remote_copy(
            src_ref=recv_z.at[slot], dst_ref=recv_z.at[slot],
            send_sem=sz_sem.at[0], recv_sem=rz_sem.at[slot],
            device_id={"row": partner},
        ).wait_recv()

    def produce(step):
        def to_send(columns, value):
            send_x[step, :, columns] = value.astype(jnp.bfloat16)

        def to_own(columns, value):
            own[step, :, columns] = value

        def to_pair_hop(columns, value):
            pair_hop_ref[:, columns] = value.astype(jnp.bfloat16)

        def to_out(columns, value):
            out_ref[1, :, columns] = value

        if step < steps - 1:
            multiply(2 * step, to_send)
            x_copy(step).start()
            multiply(2 * step + 1, to_own)
        else:
            multiply(2 * step, to_pair_hop)
            multiply(2 * step + 1, to_out)

    def last_hop(j):
        return jnp.logical_or(zd[j] == z + 1, zd[j] == z - 1)

    def add_rows(step, slot):
        @pl.loop(0, tokens // 16)
        def _(at):
            rows = pl.ds(pl.multiple_of(at * 16, 16), 16)
            own[step, rows, :] = own[step, rows, :] + recv_z[slot, rows, :].astype(jnp.float32)

    def finish(step):
        term, j = step // line, step % line
        if j < line - 1:
            inner = jnp.logical_or(
                jnp.logical_and(zd[j] > z, z > 0), jnp.logical_and(zd[j] < z, z < line - 1)
            )
            slot = term * (line + 1) + zd[j]

            @pl.when(inner)
            def _():
                wait_z(slot)
                add_rows(step, slot)

            x_copy(step).wait_recv()

            @pl.loop(0, tokens // 16)
            def _(at):
                rows = pl.ds(pl.multiple_of(at * 16, 16), 16)
                total = own[step, rows, :] + recv_x[step, rows, :].astype(jnp.float32)
                recv_x[step, rows, :] = total.astype(jnp.bfloat16)

            if term == 0:
                z_copy(step).start()
            else:
                def keep(hop_ref):
                    @pl.loop(0, tokens // 16)
                    def _(at):
                        rows = pl.ds(pl.multiple_of(at * 16, 16), 16)
                        hop_ref[rows, :] = recv_x[step, rows, :]

                @pl.when(zd[j] == z + 1)
                def _():
                    keep(up_hop_ref)

                @pl.when(zd[j] == z - 1)
                def _():
                    keep(down_hop_ref)

                @pl.when(jnp.logical_not(last_hop(j)))
                def _():
                    z_copy(step).start()
        else:
            x_copy(step).wait_recv()

            @pl.when(z > 0)
            def _():
                slot = term * (line + 1) + z
                wait_z(slot)
                add_rows(step, slot)

            @pl.when(z < line - 1)
            def _():
                slot = term * (line + 1) + line
                wait_z(slot)
                add_rows(step, slot)

            @pl.loop(0, tokens // 16)
            def _(at):
                rows = pl.ds(pl.multiple_of(at * 16, 16), 16)
                out_ref[term, rows, :] = own[step, rows, :] + recv_x[step, rows, :].astype(jnp.float32)

    lead = line + 2
    for step in range(lead):
        produce(step)
        if step == 0:
            gather(0)
    hop = 1
    for step in range(steps - 1):
        finish(step)
        if lead + step < steps:
            produce(lead + step)
        if step % 2 and hop < line:
            gather(hop)
            hop += 1
    for rest in range(hop, line):
        gather(rest)
    for step in range(steps - 1):
        x_copy(step).wait_send()
        if step < line - 1:
            z_copy(step).wait_send()
        elif step >= line:
            @pl.when(jnp.logical_not(last_hop(step - line)))
            def _():
                z_copy(step).wait_send()
    gather_end()


def reduce_terms(tokens, up_weight, gate_weight, right, rows):
    count, width = tokens.shape
    block = up_weight.shape[1] // rows
    line = rows // 2
    steps = 2 * line
    return pl.pallas_call(
        functools.partial(scatter_kernel, line),
        out_shape=(
            jax.ShapeDtypeStruct((2, count, block), jnp.float32),
            jax.ShapeDtypeStruct((count, block), jnp.bfloat16),
            jax.ShapeDtypeStruct((count, block), jnp.bfloat16),
            jax.ShapeDtypeStruct((count, block), jnp.bfloat16),
            jax.ShapeDtypeStruct((right.shape[0], rows * block), jnp.bfloat16),
        ),
        in_specs=[
            pl.BlockSpec(memory_space=pltpu.VMEM),
            pl.BlockSpec(memory_space=pl.ANY),
            pl.BlockSpec(memory_space=pl.ANY),
            pl.BlockSpec(memory_space=pl.ANY),
        ],
        out_specs=(
            pl.BlockSpec(memory_space=pltpu.VMEM),
            pl.BlockSpec(memory_space=pltpu.VMEM),
            pl.BlockSpec(memory_space=pltpu.VMEM),
            pl.BlockSpec(memory_space=pltpu.VMEM),
            pl.BlockSpec(memory_space=pl.ANY),
        ),
        scratch_shapes=[
            pltpu.VMEM((3, width, block), jnp.bfloat16),
            pltpu.VMEM((steps, count, block), jnp.bfloat16),
            pltpu.VMEM((steps, count, block), jnp.bfloat16),
            pltpu.VMEM((steps, count, block), jnp.float32),
            pltpu.VMEM((2 * (line + 1), count, block), jnp.bfloat16),
            pltpu.SemaphoreType.DMA((3,)),
            pltpu.SemaphoreType.DMA((steps,)),
            pltpu.SemaphoreType.DMA((steps,)),
            pltpu.SemaphoreType.DMA((steps,)),
            pltpu.SemaphoreType.DMA((2 * (line + 1),)),
            pltpu.SemaphoreType.DMA,
            pltpu.SemaphoreType.DMA((2,)),
            pltpu.SemaphoreType.DMA((line,)),
            pltpu.SemaphoreType.DMA((line,)),
            pltpu.SemaphoreType.DMA((line,)),
        ],
        compiler_params=pltpu.CompilerParams(
            collective_id=0, has_side_effects=True, vmem_limit_bytes=56 * 2**20
        ),
        cost_estimate=pl.CostEstimate(
            flops=4 * count * width * block * rows,
            bytes_accessed=4 * width * block * rows,
            transcendentals=0,
        ),
    )(tokens, up_weight, gate_weight, right)


def per_device(tokens, gate_weight, up_weight, gate_up_left, gate_up_right, adapter_ids):
    rank = gate_up_right.shape[2]
    rows = lax.axis_size("row")
    old_id = adapter_ids[0]
    new_id = adapter_ids[1]
    incoming_left = gate_up_left[new_id]
    outgoing_left = gate_up_left[old_id]
    gate_left_panel = jnp.concatenate(
        [incoming_left[:, :rank], -outgoing_left[:, :rank]], axis=1
    )
    right_chosen = jnp.concatenate([gate_up_right[new_id, 0], gate_up_right[old_id, 0]], axis=0)
    all_tokens = lax.all_gather(tokens, "col", axis=0, tiled=True)
    scale = float(all_tokens.shape[1] * rows) ** (-0.5)
    count = all_tokens.shape[0]
    block = up_weight.shape[1] // rows
    if rows == 8 and block % 128 == 0 and count % 16 == 0:
        panels = jnp.concatenate([gate_left_panel, incoming_left[:, rank:]], axis=1)
        low = lax.psum(
            jnp.dot(all_tokens, panels, preferred_element_type=jnp.float32), "row"
        )
        sums, up_hop, down_hop, pair_hop, right_all = reduce_terms(
            all_tokens, up_weight, gate_weight, right_chosen, rows
        )
        below = lax.ppermute(up_hop, "row", [(at, at + 2) for at in range(rows - 2)])
        above = lax.ppermute(down_hop, "row", [(at + 2, at) for at in range(rows - 2)])
        beside = lax.ppermute(pair_hop, "row", [(at, at ^ 1) for at in range(rows)])
        gate_merged = merge_panel(gate_weight, gate_left_panel, right_all)
        gate_low = jnp.dot(
            low[:, : 2 * rank], right_chosen.astype(jnp.float32),
            precision=lax.Precision.HIGHEST, preferred_element_type=jnp.float32,
        )
        gate_sum = sums[1] + beside.astype(jnp.float32)
        gate_sum = gate_sum + below.astype(jnp.float32) + above.astype(jnp.float32)
        gate_value = (gate_sum + gate_low) * scale
        up_base = sums[0] * scale
        low_term = (low[:, 2 * rank :] * scale).astype(jnp.bfloat16)
    else:
        right_all = lax.all_gather(right_chosen, "row", axis=1, tiled=True)
        gate_merged = merge_panel(gate_weight, gate_left_panel, right_all)
        low = lax.psum(
            jnp.dot(all_tokens, incoming_left[:, rank:], preferred_element_type=jnp.float32), "row"
        )
        low_term = (low * scale).astype(jnp.bfloat16)
        contract = (((0,), (1,)), ((), ()))
        gate_term = lax.dot_general(
            gate_merged, all_tokens, contract, preferred_element_type=jnp.float32
        )
        up_term = lax.dot_general(
            up_weight, all_tokens, contract, preferred_element_type=jnp.float32
        )
        sums = lax.psum_scatter(
            jnp.concatenate([gate_term, up_term], axis=1), "row", scatter_dimension=0, tiled=True
        )
        gate_value = sums[:, :count].T * scale
        up_base = sums[:, count:].T * scale
    up_value = up_base + jnp.dot(
        low_term, gate_up_right[new_id, 1], preferred_element_type=jnp.float32
    )
    hidden = (jax.nn.silu(gate_value) * up_value).astype(jnp.bfloat16)
    return (gate_merged, hidden)


def solution(mesh):
    return jax.shard_map(
        per_device,
        mesh=mesh,
        in_specs=(
            P(("groups", "col"), "row"),
            P(("groups", "row"), "col"),
            P("row", "col"),
            P(None, "row", None),
            P(None, None, None, ("col", "row")),
            P("groups"),
        ),
        out_specs=(P(("groups", "row"), "col"), P("groups", ("col", "row"))),
        check_vma=False,
    )
```
